32 devices in a mesh: dp: 4 (over y, x), tensor: 4 (over z), section: 2 (over core).
Axes of the slice: x: 2, y: 2, z: 4, core: 2. Of those that a mesh axis runs over, the one named last changes fastest.
Arguments:
- train_act: bfloat16 [2, 1024, 8192], P('section', ('dp', 'tensor')), may hold values from -6 to 6
- train_grad: bfloat16 [2, 1024, 28672], P('section', 'dp', 'tensor'), may hold values from -6 to 6
- val_act: bfloat16 [2, 16, 8192], P('section', 'dp'), may hold values from -6 to 6
- val_grad: bfloat16 [2, 16, 28672], P('section', 'dp', 'tensor'), may hold values from -6 to 6
Outputs:
- scores: float32 [1024], P(('dp', 'tensor', 'section'))
The draws below stay inside these ranges and needn't reach their ends.
All inputs are finite; a program needn't handle non-finite values.
Results may differ from the reference program's by a relative error of at most 0.0003.
Values may be sent and summed in bfloat16 or wider, within the bound.
A program may use at most 64 MiB of HBM per device.

```python
import math
import jax
import jax.numpy as jnp
from jax import lax

D = 8192
FF = 28672
LAYERS = 2
TOKENS = 1024
VTOK = 16


def block_levels(key, extent, cuts, least, top_value):
    loudness = 1.0
    for position, shards_of in cuts:
        steps = jax.random.uniform(jax.random.fold_in(jax.random.fold_in(key, 6), position), (shards_of,), jnp.float32, least / len(cuts), top_value / len(cuts))
        loudness = loudness * jnp.repeat(jnp.exp(steps), extent[position] // shards_of).reshape((-1,) + (1,) * (len(extent) - 1 - position))
    return loudness


def gaussian(rng, dims, deviation, most, shards=(), kind=jnp.bfloat16):
    array = jax.random.normal(rng, dims, jnp.float32) * deviation
    if len(shards) > 0:
        array = block_levels(rng, dims, shards, -0.22, 0.18) * array
    return jnp.clip(array, min=-most, max=most).astype(kind)


def setup_inputs(seed: int = 0) -> dict:
    seeds = jax.random.split(jax.random.key(seed), 5)
    return {
        "train_act": gaussian(seeds[0], (LAYERS, TOKENS, D), 1.0, 6.0, ((0, 2), (1, 16))),
        "train_grad": gaussian(seeds[1], (LAYERS, TOKENS, FF), 1.0, 6.0, ((0, 2), (1, 4), (2, 4))),
        "val_act": gaussian(seeds[2], (LAYERS, VTOK, D), 1.0, 6.0, ((0, 2), (1, 4))),
        "val_grad": gaussian(seeds[3], (LAYERS, VTOK, FF), 1.0, 6.0, ((0, 2), (1, 4), (2, 4))),
    }


def gram_of(left, right):
    return lax.dot_general(left, right, (((1,), (1,)), ((), ())), preferred_element_type=jnp.float32)

def reference(train_act, train_grad, val_act, val_grad):
    running = jnp.zeros((TOKENS,), jnp.float32)
    for layer in range(LAYERS):
        act_gram = gram_of(train_act[layer], val_act[layer])
        grad_gram = gram_of(train_grad[layer], val_grad[layer])
        running = running + lax.optimization_barrier(jnp.sum(act_gram * grad_gram, axis=1))
    return running / math.sqrt(D * FF * VTOK)
```

```python
import functools
import math

import jax
import jax.numpy as jnp
from jax import lax
from jax.experimental import pallas as pl
from jax.experimental.pallas import tpu as pltpu
from jax.sharding import PartitionSpec as P

LANES = 128
MIB = 1 << 20


def pieces(width, wanted):
    return max(c for c in range(1, wanted + 1) if width % (c * LANES) == 0)


def gram_of(left, right):
    return lax.dot_general(
        left, right, (((1,), (1,)), ((), ())), preferred_element_type=jnp.float32
    )


def kernel(
    sizes, factor, ta_hbm, tg_hbm, va_hbm, vg_hbm, out_ref,
    ta, tg, va, vg, ag_own, ag, ps_own, ps,
    ta_sem, tg_sem, va_sem, vg_sem, va_send, va_recv, vg_send, vg_recv,
    ag_send, ag_recv, ps_send, ps_recv,
):
    dp, tensor, section, ca, cg = sizes
    d, z, c = (lax.axis_index(a) for a in ("dp", "tensor", "section"))
    own = ta_hbm.shape[1]
    wa, wg = va.shape[2] // ca, vg.shape[2] // cg
    ranks = tensor * section

    load_va = pltpu.make_async_copy(va_hbm.at[0], va.at[d], va_sem)
    load_vg = pltpu.make_async_copy(vg_hbm.at[0], vg.at[d], vg_sem)
    load_ta = pltpu.make_async_copy(ta_hbm.at[0], ta, ta_sem)
    load_tg = pltpu.make_async_copy(tg_hbm.at[0], tg, tg_sem)
    for load in (load_va, load_vg, load_ta, load_tg):
        load.start()

    def group(r):
        dz, dc = r // section, r % section
        return {"tensor": lax.rem(z + dz, tensor), "section": lax.rem(c + dc, section)}

    barrier = pltpu.get_barrier_semaphore()
    for r in range(1, dp):
        pl.semaphore_signal(barrier, inc=1, device_id={"dp": lax.rem(d + r, dp)})
    for r in range(1, ranks):
        pl.semaphore_signal(barrier, inc=1, device_id=group(r))
    pl.semaphore_wait(barrier, dp - 1 + ranks - 1)

    def val_copy(buf, send, recv, r, k, width, slot):
        piece = buf.at[slot, :, pl.ds(k * width, width)]
        return pltpu.make_async_remote_copy(
            src_ref=piece, dst_ref=piece,
            send_sem=send.at[r - 1, k], recv_sem=recv.at[r - 1, k],
            device_id={"dp": lax.rem(d + r, dp)},
        )

    load_va.wait()
    for k in range(ca):
        for r in range(1, dp):
            val_copy(va, va_send, va_recv, r, k, wa, d).start()
    load_vg.wait()
    for k in range(cg):
        for r in range(1, dp):
            val_copy(vg, vg_send, vg_recv, r, k, wg, d).start()

    def gram(buf, send, recv, train, count, width):
        total = None
        for k in range(count):
            for r in range(1, dp):
                val_copy(buf, send, recv, r, k, width, lax.rem(d + dp - r, dp)).wait_recv()
            cols = pl.ds(k * width, width)
            left = jnp.concatenate([buf[j, :, cols] for j in range(dp)], axis=0)
            term = gram_of(left, train[:, cols])
            total = term if total is None else total + term
        return total

    load_ta.wait()
    act = gram(va, va_send, va_recv, ta, ca, wa)
    ag_own[...] = jnp.zeros_like(ag_own)
    ag_own[:, 0:own] = act

    def act_copy(r, slot):
        return pltpu.make_async_remote_copy(
            src_ref=ag_own, dst_ref=ag.at[slot],
            send_sem=ag_send.at[r - 1], recv_sem=ag_recv.at[r - 1],
            device_id={"tensor": lax.rem(z + r, tensor)},
        )

    for r in range(1, tensor):
        act_copy(r, z).start()
    ag[z] = ag_own[...]

    load_tg.wait()
    grad = gram(vg, vg_send, vg_recv, tg, cg, wg)

    for r in range(1, tensor):
        act_copy(r, lax.rem(z + tensor - r, tensor)).wait_recv()
    act_all = jnp.concatenate([ag[j, :, 0:own] for j in range(tensor)], axis=1)
    ps_own[...] = jnp.sum(act_all * grad, axis=0, keepdims=True) * factor

    def score_copy(r, slot):
        return pltpu.make_async_remote_copy(
            src_ref=ps_own, dst_ref=ps.at[slot],
            send_sem=ps_send.at[r - 1], recv_sem=ps_recv.at[r - 1],
            device_id=group(r),
        )

    for r in range(1, ranks):
        score_copy(r, r - 1).start()
    total = ps_own[...]
    for r in range(1, ranks):
        score_copy(r, r - 1).wait_recv()
        total = total + ps[r - 1]
    share = total.shape[1] // ranks
    mine = z * section + c
    result = total[:, 0:share]
    for b in range(1, ranks):
        result = jnp.where(mine == b, total[:, b * share : (b + 1) * share], result)
    out_ref[...] = result

    for r in range(1, dp):
        for k in range(ca):
            val_copy(va, va_send, va_recv, r, k, wa, d).wait_send()
        for k in range(cg):
            val_copy(vg, vg_send, vg_recv, r, k, wg, d).wait_send()
    for r in range(1, tensor):
        act_copy(r, z).wait_send()
    for r in range(1, ranks):
        score_copy(r, r - 1).wait_send()


def solution(mesh):
    dp, tensor, section = (mesh.shape[a] for a in ("dp", "tensor", "section"))

    def local(train_act, train_grad, val_act, val_grad):
        own, width = train_act.shape[1:]
        tokens, hidden = train_grad.shape[1:]
        val = val_act.shape[1]
        factor = 1.0 / math.sqrt(width * hidden * tensor * val * dp)
        ca, cg = pieces(width, 2), pieces(hidden, 4)
        ranks = tensor * section
        share = tokens // ranks
        own_lanes = -(-own // LANES) * LANES
        dma = pltpu.SemaphoreType.DMA
        bf16, f32 = jnp.bfloat16, jnp.float32
        scores = pl.pallas_call(
            functools.partial(kernel, (dp, tensor, section, ca, cg), factor),
            out_shape=jax.ShapeDtypeStruct((1, share), f32),
            in_specs=[pl.BlockSpec(memory_space=pl.ANY)] * 4,
            out_specs=pl.BlockSpec(memory_space=pltpu.VMEM),
            scratch_shapes=[
                pltpu.VMEM((own, width), bf16),
                pltpu.VMEM((tokens, hidden), bf16),
                pltpu.VMEM((dp, val, width), bf16),
                pltpu.VMEM((dp, val, hidden), bf16),
                pltpu.VMEM((val * dp, own_lanes), f32),
                pltpu.VMEM((tensor, val * dp, own_lanes), f32),
                pltpu.VMEM((1, tokens), f32),
                pltpu.VMEM((ranks - 1, 1, tokens), f32),
                dma, dma, dma, dma,
                dma((dp - 1, ca)), dma((dp - 1, ca)),
                dma((dp - 1, cg)), dma((dp - 1, cg)),
                dma((tensor - 1,)), dma((tensor - 1,)),
                dma((ranks - 1,)), dma((ranks - 1,)),
            ],
            compiler_params=pltpu.CompilerParams(
                collective_id=0, has_side_effects=True, vmem_limit_bytes=56 * MIB
            ),
        )(train_act, train_grad, val_act, val_grad)
        return scores.reshape(share)

    in_specs = (
        P("section", ("dp", "tensor"), None),
        P("section", "dp", "tensor"),
        P("section", "dp", None),
        P("section", "dp", "tensor"),
    )
    out_specs = P(("dp", "tensor", "section"))
    return jax.shard_map(local, mesh=mesh, in_specs=in_specs, out_specs=out_specs, check_vma=False)
```

```python
import functools
import math

import jax
import jax.numpy as jnp
from jax import lax
from jax.experimental import pallas as pl
from jax.experimental.pallas import tpu as pltpu
from jax.sharding import PartitionSpec as P

LANES = 128
MIB = 1 << 20


def pieces(width, wanted):
    return max(c for c in range(1, wanted + 1) if width % (c * LANES) == 0)


def gram_of(left, right):
    return lax.dot_general(
        left, right, (((1,), (1,)), ((), ())), preferred_element_type=jnp.float32
    )


def peer(me, r):
    bit = 1
    while bit <= r:
        if r & bit:
            me = me + bit * (1 - 2 * ((me // bit) % 2))
        bit *= 2
    return me


def kernel(
    sizes, factor, ta_hbm, tg_hbm, va_hbm, vg_hbm, out_ref,
    ta, tg, va, vg, gz_own, gz, ps_own, ps,
    ta_sem, tg_sem, va_sem, vg_sem, va_send, va_recv, vg_send, vg_recv,
    gz_send, gz_recv, ps_send, ps_recv, dp_relay, z_relay,
):
    dp, tensor, section, ca, cg = sizes
    d, z, c = (lax.axis_index(a) for a in ("dp", "tensor", "section"))
    own = ta_hbm.shape[1]
    wa, wg = va.shape[2] // ca, vg.shape[2] // cg
    square = dp == 4
    near = (1, 2) if square else tuple(range(1, dp))
    far = (3,) if square else ()

    def dp_peer(r):
        if square:
            return peer(d, r), peer(d, r)
        return lax.rem(d + r, dp), lax.rem(d + dp - r, dp)

    def chain(signal):
        for step, there in ((-1, z > 0), (1, z < tensor - 1)):
            pl.when(there)(functools.partial(signal, {"tensor": z + step}))
        return jnp.where(z > 0, 1, 0) + jnp.where(z < tensor - 1, 1, 0)

    load_va = pltpu.make_async_copy(va_hbm.at[0], va.at[d], va_sem)
    load_vg = pltpu.make_async_copy(vg_hbm.at[0], vg.at[d], vg_sem)
    load_ta = pltpu.make_async_copy(ta_hbm.at[0], ta, ta_sem)
    load_tg = pltpu.make_async_copy(tg_hbm.at[0], tg, tg_sem)
    for load in (load_vg, load_va, load_tg, load_ta):
        load.start()

    barrier = pltpu.get_barrier_semaphore()
    greeted = chain(lambda there: pl.semaphore_signal(barrier, inc=1, device_id=there))
    for r in near:
        pl.semaphore_signal(barrier, inc=1, device_id={"dp": dp_peer(r)[0]})
    for r in range(1, section):
        pl.semaphore_signal(barrier, inc=1, device_id={"section": lax.rem(c + r, section)})
    pl.semaphore_wait(barrier, greeted + len(near) + section - 1)

    def val_copy(buf, send, recv, r, k, width, incoming=False):
        piece = buf.at[dp_peer(r)[1] if incoming else d, :, pl.ds(k * width, width)]
        return pltpu.make_async_remote_copy(
            src_ref=piece, dst_ref=piece,
            send_sem=send.at[r - 1, k], recv_sem=recv.at[r - 1, k],
            device_id={"dp": dp_peer(r)[0]},
        )

    if square:
        pl.semaphore_signal(dp_relay, inc=1, device_id={"dp": peer(d, 1)})
    if tensor > 2:
        chain(lambda there: pl.semaphore_signal(z_relay.at[0], inc=1, device_id=there))
    load_vg.wait()
    for k in range(cg):
        for r in near:
            val_copy(vg, vg_send, vg_recv, r, k, wg).start()
    if square:
        pl.semaphore_wait(dp_relay, 1)
    for k in range(cg):
        for r in far:
            val_copy(vg, vg_send, vg_recv, r, k, wg).start()
    load_va.wait()
    for k in range(ca):
        for r in near + far:
            val_copy(va, va_send, va_recv, r, k, wa).start()
    for s in range(tensor - 2):
        pl.semaphore_wait(z_relay.at[s], greeted)
        if s < tensor - 3:
            chain(lambda there, s=s: pl.semaphore_signal(z_relay.at[s + 1], inc=1, device_id=there))
    gz_own[...] = jnp.zeros_like(gz_own)
    ps_own[...] = jnp.zeros_like(ps_own)

    def gram(buf, send, recv, train, count, width):
        total = None
        for k in range(count):
            for r in near + far:
                val_copy(buf, send, recv, r, k, width, incoming=True).wait_recv()
            cols = pl.ds(k * width, width)
            left = jnp.concatenate([buf[j, :, cols] for j in range(dp)], axis=0)
            term = gram_of(left, train[:, cols])
            total = term if total is None else total + term
        return total

    load_tg.wait()
    grad = gram(vg, vg_send, vg_recv, tg, cg, wg)
    for j in range(tensor):
        gz_own[j, :, 0:own] = grad[:, j * own : (j + 1) * own]

    def grad_copy(r):
        there = lax.rem(z + r, tensor)
        return pltpu.make_async_remote_copy(
            src_ref=gz_own.at[there], dst_ref=gz.at[r - 1],
            send_sem=gz_send.at[r - 1], recv_sem=gz_recv.at[r - 1],
            device_id={"tensor": there},
        )

    for r in range(1, tensor):
        grad_copy(r).start()

    load_ta.wait()
    act = gram(va, va_send, va_recv, ta, ca, wa)

    grad_sum = gz_own[z]
    for r in range(1, tensor):
        grad_copy(r).wait_recv()
        grad_sum = grad_sum + gz[r - 1]
    scores = jnp.sum(act * grad_sum[:, 0:own], axis=0, keepdims=True) * factor
    ps_own[:, 0:own] = scores

    def score_copy(r):
        return pltpu.make_async_remote_copy(
            src_ref=ps_own, dst_ref=ps.at[r - 1],
            send_sem=ps_send.at[r - 1], recv_sem=ps_recv.at[r - 1],
            device_id={"section": lax.rem(c + r, section)},
        )

    for r in range(1, section):
        score_copy(r).start()
    for r in range(1, section):
        score_copy(r).wait_recv()
        scores = scores + ps[r - 1][:, 0:own]
    share = own // section
    result = scores[:, 0:share]
    for b in range(1, section):
        result = jnp.where(c == b, scores[:, b * share : (b + 1) * share], result)
    out_ref[...] = result

    for r in near + far:
        for k in range(cg):
            val_copy(vg, vg_send, vg_recv, r, k, wg).wait_send()
        for k in range(ca):
            val_copy(va, va_send, va_recv, r, k, wa).wait_send()
    for r in range(1, tensor):
        grad_copy(r).wait_send()
    for r in range(1, section):
        score_copy(r).wait_send()


def solution(mesh):
    dp, tensor, section = (mesh.shape[a] for a in ("dp", "tensor", "section"))

    def local(train_act, train_grad, val_act, val_grad):
        own, width = train_act.shape[1:]
        tokens, hidden = train_grad.shape[1:]
        val = val_act.shape[1]
        factor = 1.0 / math.sqrt(width * hidden * tensor * val * dp)
        ca, cg = pieces(width, 1), pieces(hidden, 2)
        share = tokens // (tensor * section)
        own_lanes = -(-own // LANES) * LANES
        dma = pltpu.SemaphoreType.DMA
        bf16, f32 = jnp.bfloat16, jnp.float32
        scores = pl.pallas_call(
            functools.partial(kernel, (dp, tensor, section, ca, cg), factor),
            out_shape=jax.ShapeDtypeStruct((1, share), f32),
            in_specs=[pl.BlockSpec(memory_space=pl.ANY)] * 4,
            out_specs=pl.BlockSpec(memory_space=pltpu.VMEM),
            scratch_shapes=[
                pltpu.VMEM((own, width), bf16),
                pltpu.VMEM((tokens, hidden), bf16),
                pltpu.VMEM((dp, val, width), bf16),
                pltpu.VMEM((dp, val, hidden), bf16),
                pltpu.VMEM((tensor, val * dp, own_lanes), f32),
                pltpu.VMEM((tensor - 1, val * dp, own_lanes), f32),
                pltpu.VMEM((1, own_lanes), f32),
                pltpu.VMEM((section - 1, 1, own_lanes), f32),
                dma, dma, dma, dma,
                dma((dp - 1, ca)), dma((dp - 1, ca)),
                dma((dp - 1, cg)), dma((dp - 1, cg)),
                dma((tensor - 1,)), dma((tensor - 1,)),
                dma((section - 1,)), dma((section - 1,)),
                pltpu.SemaphoreType.REGULAR,
                pltpu.SemaphoreType.REGULAR((max(tensor - 2, 1),)),
            ],
            compiler_params=pltpu.CompilerParams(
                collective_id=0, has_side_effects=True, vmem_limit_bytes=56 * MIB
            ),
        )(train_act, train_grad, val_act, val_grad)
        return scores.reshape(share)

    in_specs = (
        P("section", ("dp", "tensor"), None),
        P("section", "dp", "tensor"),
        P("section", "dp", None),
        P("section", "dp", "tensor"),
    )
    out_specs = P(("dp", "tensor", "section"))
    return jax.shard_map(local, mesh=mesh, in_specs=in_specs, out_specs=out_specs, check_vma=False)
```

```python
import functools
import math

import jax
import jax.numpy as jnp
from jax import lax
from jax.experimental import pallas as pl
from jax.experimental.pallas import tpu as pltpu
from jax.sharding import PartitionSpec as P

LANES = 128
MIB = 1 << 20


def pieces(width, wanted):
    return max(c for c in range(1, wanted + 1) if width % (c * LANES) == 0)


def gram_of(left, right):
    return lax.dot_general(
        left, right, (((1,), (1,)), ((), ())), preferred_element_type=jnp.float32
    )


def peer(me, r):
    bit = 1
    while bit <= r:
        if r & bit:
            me = me + bit * (1 - 2 * ((me // bit) % 2))
        bit *= 2
    return me


def kernel(
    sizes, factor, ta_hbm, tg_hbm, va_hbm, vg_hbm, out_ref,
    ta, tg, va, vg, gz_own, gz, ps_own, ps,
    ta_sem, tg_sem, va_sem, vg_sem, va_send, va_recv, vg_send, vg_recv,
    gz_send, gz_recv, ps_send, ps_recv, dp_relay, z_relay,
):
    dp, tensor, section, ca, cg = sizes
    d, z, c = (lax.axis_index(a) for a in ("dp", "tensor", "section"))
    own = ta_hbm.shape[1]
    wa, wg = va.shape[2] // ca, vg.shape[2] // cg
    square = dp == 4
    near = (1, 2) if square else tuple(range(1, dp))
    far = (3,) if square else ()

    def dp_peer(r):
        if square:
            return peer(d, r), peer(d, r)
        return lax.rem(d + r, dp), lax.rem(d + dp - r, dp)

    def chain(signal):
        for step, there in ((-1, z > 0), (1, z < tensor - 1)):
            pl.when(there)(functools.partial(signal, {"tensor": z + step}))
        return jnp.where(z > 0, 1, 0) + jnp.where(z < tensor - 1, 1, 0)

    load_va = pltpu.make_async_copy(va_hbm.at[0], va.at[d], va_sem)
    load_vg = pltpu.make_async_copy(vg_hbm.at[0], vg.at[d], vg_sem)
    load_ta = pltpu.make_async_copy(ta_hbm.at[0], ta, ta_sem)
    load_tg = pltpu.make_async_copy(tg_hbm.at[0], tg, tg_sem)

    barrier = pltpu.get_barrier_semaphore()
    greeted = chain(lambda there: pl.semaphore_signal(barrier, inc=1, device_id=there))
    for r in near:
        pl.semaphore_signal(barrier, inc=1, device_id={"dp": dp_peer(r)[0]})
    for r in range(1, section):
        pl.semaphore_signal(barrier, inc=1, device_id={"section": lax.rem(c + r, section)})
    for load in (load_vg, load_va, load_tg, load_ta):
        load.start()
    pl.semaphore_wait(barrier, greeted + len(near) + section - 1)

    def val_copy(buf, send, recv, r, k, width, incoming=False):
        piece = buf.at[dp_peer(r)[1] if incoming else d, :, pl.ds(k * width, width)]
        return pltpu.make_async_remote_copy(
            src_ref=piece, dst_ref=piece,
            send_sem=send.at[r - 1, k], recv_sem=recv.at[r - 1, k],
            device_id={"dp": dp_peer(r)[0]},
        )

    if square:
        pl.semaphore_signal(dp_relay, inc=1, device_id={"dp": peer(d, 1)})
    if tensor > 2:
        chain(lambda there: pl.semaphore_signal(z_relay.at[0], inc=1, device_id=there))
    load_vg.wait()
    for k in range(cg):
        for r in near:
            val_copy(vg, vg_send, vg_recv, r, k, wg).start()
    if square:
        pl.semaphore_wait(dp_relay, 1)
    for k in range(cg):
        for r in far:
            val_copy(vg, vg_send, vg_recv, r, k, wg).start()
    load_va.wait()
    for k in range(ca):
        for r in near + far:
            val_copy(va, va_send, va_recv, r, k, wa).start()
    for s in range(tensor - 2):
        pl.semaphore_wait(z_relay.at[s], greeted)
        if s < tensor - 3:
            chain(lambda there, s=s: pl.semaphore_signal(z_relay.at[s + 1], inc=1, device_id=there))
    gz_own[...] = jnp.zeros_like(gz_own)
    ps_own[...] = jnp.zeros_like(ps_own)

    def gram(buf, send, recv, train, count, width):
        total = None
        for k in range(count):
            for r in near + far:
                val_copy(buf, send, recv, r, k, width, incoming=True).wait_recv()
            cols = pl.ds(k * width, width)
            left = jnp.concatenate([buf[j, :, cols] for j in range(dp)], axis=0)
            term = gram_of(left, train[:, cols])
            total = term if total is None else total + term
        return total

    load_tg.wait()
    grad = gram(vg, vg_send, vg_recv, tg, cg, wg)
    for j in range(tensor):
        gz_own[j, :, 0:own] = grad[:, j * own : (j + 1) * own]

    def grad_copy(r):
        there = lax.rem(z + r, tensor)
        return pltpu.make_async_remote_copy(
            src_ref=gz_own.at[there], dst_ref=gz.at[r - 1],
            send_sem=gz_send.at[r - 1], recv_sem=gz_recv.at[r - 1],
            device_id={"tensor": there},
        )

    for r in range(1, tensor):
        grad_copy(r).start()

    load_ta.wait()
    act = gram(va, va_send, va_recv, ta, ca, wa)

    grad_sum = gz_own[z]
    for r in range(1, tensor):
        grad_copy(r).wait_recv()
        grad_sum = grad_sum + gz[r - 1]
    scores = jnp.sum(act * grad_sum[:, 0:own], axis=0, keepdims=True) * factor
    ps_own[:, 0:own] = scores

    def score_copy(r):
        return pltpu.make_async_remote_copy(
            src_ref=ps_own, dst_ref=ps.at[r - 1],
            send_sem=ps_send.at[r - 1], recv_sem=ps_recv.at[r - 1],
            device_id={"section": lax.rem(c + r, section)},
        )

    for r in range(1, section):
        score_copy(r).start()
    for r in range(1, section):
        score_copy(r).wait_recv()
        scores = scores + ps[r - 1][:, 0:own]
    share = own // section
    result = scores[:, 0:share]
    for b in range(1, section):
        result = jnp.where(c == b, scores[:, b * share : (b + 1) * share], result)
    out_ref[...] = result

    for r in near + far:
        for k in range(cg):
            val_copy(vg, vg_send, vg_recv, r, k, wg).wait_send()
        for k in range(ca):
            val_copy(va, va_send, va_recv, r, k, wa).wait_send()
    for r in range(1, tensor):
        grad_copy(r).wait_send()
    for r in range(1, section):
        score_copy(r).wait_send()


def solution(mesh):
    dp, tensor, section = (mesh.shape[a] for a in ("dp", "tensor", "section"))

    def local(train_act, train_grad, val_act, val_grad):
        own, width = train_act.shape[1:]
        tokens, hidden = train_grad.shape[1:]
        val = val_act.shape[1]
        factor = 1.0 / math.sqrt(width * hidden * tensor * val * dp)
        ca, cg = pieces(width, 1), pieces(hidden, 2)
        share = tokens // (tensor * section)
        own_lanes = -(-own // LANES) * LANES
        dma = pltpu.SemaphoreType.DMA
        bf16, f32 = jnp.bfloat16, jnp.float32
        scores = pl.pallas_call(
            functools.partial(kernel, (dp, tensor, section, ca, cg), factor),
            out_shape=jax.ShapeDtypeStruct((1, share), f32),
            in_specs=[pl.BlockSpec(memory_space=pl.ANY)] * 4,
            out_specs=pl.BlockSpec(memory_space=pltpu.VMEM),
            scratch_shapes=[
                pltpu.VMEM((own, width), bf16),
                pltpu.VMEM((tokens, hidden), bf16),
                pltpu.VMEM((dp, val, width), bf16),
                pltpu.VMEM((dp, val, hidden), bf16),
                pltpu.VMEM((tensor, val * dp, own_lanes), f32),
                pltpu.VMEM((tensor - 1, val * dp, own_lanes), f32),
                pltpu.VMEM((1, own_lanes), f32),
                pltpu.VMEM((section - 1, 1, own_lanes), f32),
                dma, dma, dma, dma,
                dma((dp - 1, ca)), dma((dp - 1, ca)),
                dma((dp - 1, cg)), dma((dp - 1, cg)),
                dma((tensor - 1,)), dma((tensor - 1,)),
                dma((section - 1,)), dma((section - 1,)),
                pltpu.SemaphoreType.REGULAR,
                pltpu.SemaphoreType.REGULAR((max(tensor - 2, 1),)),
            ],
            compiler_params=pltpu.CompilerParams(
                collective_id=0, has_side_effects=True, vmem_limit_bytes=56 * MIB
            ),
        )(train_act, train_grad, val_act, val_grad)
        return scores.reshape(share)

    in_specs = (
        P("section", ("dp", "tensor"), None),
        P("section", "dp", "tensor"),
        P("section", "dp", None),
        P("section", "dp", "tensor"),
    )
    out_specs = P(("dp", "tensor", "section"))
    return jax.shard_map(local, mesh=mesh, in_specs=in_specs, out_specs=out_specs, check_vma=False)
```

```python
import functools
import math

import jax
import jax.numpy as jnp
from jax import lax
from jax.experimental import pallas as pl
from jax.experimental.pallas import tpu as pltpu
from jax.sharding import PartitionSpec as P

LANES = 128
MIB = 1 << 20


def pieces(width, wanted):
    return max(c for c in range(1, wanted + 1) if width % (c * LANES) == 0)


def gram_of(left, right):
    return lax.dot_general(
        left, right, (((1,), (1,)), ((), ())), preferred_element_type=jnp.float32
    )


def peer(me, r):
    bit = 1
    while bit <= r:
        if r & bit:
            me = me + bit * (1 - 2 * ((me // bit) % 2))
        bit *= 2
    return me


def kernel(
    sizes, factor, ta_hbm, tg_hbm, va_hbm, vg_hbm, out_ref,
    ta, tg, va, vg, gz_own, gz, ps_own, ps,
    ta_sem, tg_sem, va_sem, vg_sem, va_send, va_recv, vg_send, vg_recv,
    gz_send, gz_recv, ps_send, ps_recv, dp_relay, z_relay,
):
    dp, tensor, section, ca, cg = sizes
    d, z, c = (lax.axis_index(a) for a in ("dp", "tensor", "section"))
    own = ta_hbm.shape[1]
    wa, wg = va.shape[2] // ca, vg.shape[2] // cg
    square = dp == 4
    near = (1, 2) if square else tuple(range(1, dp))
    far = (3,) if square else ()

    def dp_peer(r):
        if square:
            return peer(d, r), peer(d, r)
        return lax.rem(d + r, dp), lax.rem(d + dp - r, dp)

    def chain(signal):
        for step, there in ((-1, z > 0), (1, z < tensor - 1)):
            pl.when(there)(functools.partial(signal, {"tensor": z + step}))
        return jnp.where(z > 0, 1, 0) + jnp.where(z < tensor - 1, 1, 0)

    load_va = pltpu.make_async_copy(va_hbm.at[0], va.at[d], va_sem)
    load_vg = pltpu.make_async_copy(vg_hbm.at[0], vg.at[d], vg_sem)
    load_ta = pltpu.make_async_copy(ta_hbm.at[0], ta, ta_sem)
    load_tg = pltpu.make_async_copy(tg_hbm.at[0], tg, tg_sem)

    barrier = pltpu.get_barrier_semaphore()
    for r in near:
        pl.semaphore_signal(barrier, inc=1, device_id={"dp": dp_peer(r)[0]})
    greeted = chain(lambda there: pl.semaphore_signal(barrier, inc=1, device_id=there))
    for r in range(1, section):
        pl.semaphore_signal(barrier, inc=1, device_id={"section": lax.rem(c + r, section)})
    for load in (load_vg, load_va, load_tg, load_ta):
        load.start()
    pl.semaphore_wait(barrier, greeted + len(near) + section - 1)

    def val_copy(buf, send, recv, r, k, width, incoming=False):
        piece = buf.at[dp_peer(r)[1] if incoming else d, :, pl.ds(k * width, width)]
        return pltpu.make_async_remote_copy(
            src_ref=piece, dst_ref=piece,
            send_sem=send.at[r - 1, k], recv_sem=recv.at[r - 1, k],
            device_id={"dp": dp_peer(r)[0]},
        )

    if square:
        pl.semaphore_signal(dp_relay, inc=1, device_id={"dp": peer(d, 1)})
    if tensor > 2:
        chain(lambda there: pl.semaphore_signal(z_relay.at[0], inc=1, device_id=there))
    load_vg.wait()
    for k in range(cg):
        for r in near:
            val_copy(vg, vg_send, vg_recv, r, k, wg).start()
    if square:
        pl.semaphore_wait(dp_relay, 1)
    for k in range(cg):
        for r in far:
            val_copy(vg, vg_send, vg_recv, r, k, wg).start()
    load_va.wait()
    for k in range(ca):
        for r in near:
            val_copy(va, va_send, va_recv, r, k, wa).start()
    for s in range(tensor - 2):
        pl.semaphore_wait(z_relay.at[s], greeted)
        if s < tensor - 3:
            chain(lambda there, s=s: pl.semaphore_signal(z_relay.at[s + 1], inc=1, device_id=there))
    gz_own[...] = jnp.zeros_like(gz_own)
    ps_own[...] = jnp.zeros_like(ps_own)

    def gram(buf, send, recv, train, count, width):
        total = None
        for k in range(count):
            for r in near + far:
                if not (square and buf is va and r == near[k % 2]):
                    val_copy(buf, send, recv, r, k, width, incoming=True).wait_recv()
            cols = pl.ds(k * width, width)
            left = jnp.concatenate([buf[j, :, cols] for j in range(dp)], axis=0)
            term = gram_of(left, train[:, cols])
            total = term if total is None else total + term
        return total

    load_tg.wait()
    grad = gram(vg, vg_send, vg_recv, tg, cg, wg)
    for j in range(tensor):
        gz_own[j, :, 0:own] = grad[:, j * own : (j + 1) * own]

    def grad_copy(r):
        there = lax.rem(z + r, tensor)
        return pltpu.make_async_remote_copy(
            src_ref=gz_own.at[there], dst_ref=gz.at[r - 1],
            send_sem=gz_send.at[r - 1], recv_sem=gz_recv.at[r - 1],
            device_id={"tensor": there},
        )

    for r in range(1, tensor):
        grad_copy(r).start()

    def passed_on(k):
        via = near[k % 2]
        piece = va.at[dp_peer(via)[1], :, pl.ds(k * wa, wa)]
        return pltpu.make_async_remote_copy(
            src_ref=piece, dst_ref=piece,
            send_sem=va_send.at[2, k], recv_sem=va_recv.at[2, k],
            device_id={"dp": dp_peer(3 - via)[0]},
        )

    if square:
        for k in range(ca):
            val_copy(va, va_send, va_recv, near[k % 2], k, wa, incoming=True).wait_recv()
            passed_on(k).start()

    load_ta.wait()
    act = gram(va, va_send, va_recv, ta, ca, wa)

    grad_sum = gz_own[z]
    for r in range(1, tensor):
        grad_copy(r).wait_recv()
        grad_sum = grad_sum + gz[r - 1]
    scores = jnp.sum(act * grad_sum[:, 0:own], axis=0, keepdims=True) * factor
    ps_own[:, 0:own] = scores

    def score_copy(r):
        return pltpu.make_async_remote_copy(
            src_ref=ps_own, dst_ref=ps.at[r - 1],
            send_sem=ps_send.at[r - 1], recv_sem=ps_recv.at[r - 1],
            device_id={"section": lax.rem(c + r, section)},
        )

    for r in range(1, section):
        score_copy(r).start()
    for r in range(1, section):
        score_copy(r).wait_recv()
        scores = scores + ps[r - 1][:, 0:own]
    share = own // section
    result = scores[:, 0:share]
    for b in range(1, section):
        result = jnp.where(c == b, scores[:, b * share : (b + 1) * share], result)
    out_ref[...] = result

    for r in near + far:
        for k in range(cg):
            val_copy(vg, vg_send, vg_recv, r, k, wg).wait_send()
        for k in range(ca):
            val_copy(va, va_send, va_recv, r, k, wa).wait_send()
    for r in range(1, tensor):
        grad_copy(r).wait_send()
    for r in range(1, section):
        score_copy(r).wait_send()


def solution(mesh):
    dp, tensor, section = (mesh.shape[a] for a in ("dp", "tensor", "section"))

    def local(train_act, train_grad, val_act, val_grad):
        own, width = train_act.shape[1:]
        tokens, hidden = train_grad.shape[1:]
        val = val_act.shape[1]
        factor = 1.0 / math.sqrt(width * hidden * tensor * val * dp)
        ca, cg = pieces(width, 2), pieces(hidden, 2)
        share = tokens // (tensor * section)
        own_lanes = -(-own // LANES) * LANES
        dma = pltpu.SemaphoreType.DMA
        bf16, f32 = jnp.bfloat16, jnp.float32
        scores = pl.pallas_call(
            functools.partial(kernel, (dp, tensor, section, ca, cg), factor),
            out_shape=jax.ShapeDtypeStruct((1, share), f32),
            in_specs=[pl.BlockSpec(memory_space=pl.ANY)] * 4,
            out_specs=pl.BlockSpec(memory_space=pltpu.VMEM),
            scratch_shapes=[
                pltpu.VMEM((own, width), bf16),
                pltpu.VMEM((tokens, hidden), bf16),
                pltpu.VMEM((dp, val, width), bf16),
                pltpu.VMEM((dp, val, hidden), bf16),
                pltpu.VMEM((tensor, val * dp, own_lanes), f32),
                pltpu.VMEM((tensor - 1, val * dp, own_lanes), f32),
                pltpu.VMEM((1, own_lanes), f32),
                pltpu.VMEM((section - 1, 1, own_lanes), f32),
                dma, dma, dma, dma,
                dma((dp - 1, ca)), dma((dp - 1, ca)),
                dma((dp - 1, cg)), dma((dp - 1, cg)),
                dma((tensor - 1,)), dma((tensor - 1,)),
                dma((section - 1,)), dma((section - 1,)),
                pltpu.SemaphoreType.REGULAR,
                pltpu.SemaphoreType.REGULAR((max(tensor - 2, 1),)),
            ],
            compiler_params=pltpu.CompilerParams(
                collective_id=0, has_side_effects=True, vmem_limit_bytes=56 * MIB
            ),
        )(train_act, train_grad, val_act, val_grad)
        return scores.reshape(share)

    in_specs = (
        P("section", ("dp", "tensor"), None),
        P("section", "dp", "tensor"),
        P("section", "dp", None),
        P("section", "dp", "tensor"),
    )
    out_specs = P(("dp", "tensor", "section"))
    return jax.shard_map(local, mesh=mesh, in_specs=in_specs, out_specs=out_specs, check_vma=False)
```
